256 devices in a mesh: ctx: 16 (over z_lo, x), tp: 16 (over y, z_hi, core).
Axes of the slice: x: 4, y: 4, z: 8 (z_hi: 2, z_lo: 4; z = z_hi * 4 + z_lo), core: 2. Of those that a mesh axis runs over, the one named last changes fastest.
Arguments:
- query_rows: bfloat16 [6144, 8192], P('ctx', 'tp'), may hold values from -5 to 5
- key_rows: bfloat16 [6144, 1024], P('ctx'), may hold values from -5 to 5
- value_rows: bfloat16 [6144, 1024], P('ctx'), may hold values from -18 to 18
- out_weight: bfloat16 [8192, 16384], P('tp', 'ctx'), may hold values from -0.25 to 0.25
- block_order: int32 [32], replicated, may hold values from 0 to 31, as said below
- doc_lengths: int32 [4], replicated, may hold values from 1 to 3072, 6144 in all
Outputs:
- projected: bfloat16 [6144, 16384], P(('ctx', 'tp'))
The draws below stay inside these ranges and needn't reach their ends.
Inputs may be any that keep to these rules, and one draw needn't show every extreme that they name: A permutation of 0 to 31 in which block_order[2 c] + block_order[2 c + 1] = 31 for every c.
All inputs are finite; a program needn't handle non-finite values.
Results may differ from the reference program's by a relative error of at most 0.017.
Values may be sent and summed in bfloat16 or wider, within the bound.
No kernel may reach another device: no remote copies, remote signals or barrier semaphores. Data moves between devices by JAX's collectives and lax.ppermute only.
A program may use at most 128 MiB of HBM per device.

```python
import math
import jax
import jax.numpy as jnp
import numpy as np
from jax import lax

D = 16384
HQ = 64
KVH = 8
HD = 128
NDOC = 4
GROUP = 8
HALF = 192
SEQ = 6144
N_CTX = 16
N_TP = 16


def drawn_keys(key):
    return jnp.clip(jax.random.normal(key, (SEQ, KVH * HD), jnp.float32), -4.0, 4.0)


def draw_key_rows(key, part):
    common = drawn_keys(key)
    return common.astype(jnp.bfloat16)


def draw_query_rows(key, part):
    key = jax.random.fold_in(key, 4)
    queries = jnp.clip(jax.random.normal(key, (SEQ, HQ * HD), jnp.float32), -4.0, 4.0)
    return queries.astype(jnp.bfloat16)


def draw_block_order(key, part):
    key = jax.random.fold_in(key, 5)
    pairing = jax.random.permutation(jax.random.fold_in(key, 1), N_CTX).astype(jnp.int32)
    flipped = jax.random.randint(jax.random.fold_in(key, 2), (N_CTX,), 0, 2)
    leading = jnp.where(flipped == 1, 2 * N_CTX - 1 - pairing, pairing)
    trailing = 2 * N_CTX - 1 - leading
    return jnp.stack([leading, trailing], axis=1).reshape(2 * N_CTX).astype(jnp.int32)


def steps_of(key, shape, pieces, smallest, top_value):
    gain, own = 1.0, jax.random.fold_in(key, 6)
    for dim, shards_of in pieces:
        draws = jnp.exp(jax.random.uniform(jax.random.fold_in(own, dim), (shards_of,), jnp.float32, smallest / len(pieces), top_value / len(pieces)))
        gain = gain * jnp.repeat(draws, shape[dim] // shards_of).reshape([-1 if axis == dim else 1 for axis in range(len(shape))])
    return gain


def profile(number_of, total, bound, skew):
    weights = [(1 << 20) // math.isqrt(rank ** skew) + 1 for rank in range(2, number_of + 1)]
    surplus, counts = total - bound - (number_of - 1), [1] * (number_of - 1)
    while surplus > 0:
        movable = [i for i in range(number_of - 1) if counts[i] < bound]
        whole, left = sum([weights[i] for i in movable]), surplus
        for i in movable:
            extra = min(bound - counts[i], max(1, left * weights[i] // whole), surplus)
            counts[i] = counts[i] + extra
            surplus = surplus - extra
    return np.array([bound] + counts)


def uneven(own_key, number_of, total, bound, skew):
    if number_of == 2:
        one = jax.random.randint(own_key, (), max(1, total - bound), min(bound, total - 1) + 1)
        return jnp.stack([one, total - one])
    lengths = jnp.asarray(profile(number_of, total, bound, skew), jnp.int32)
    couples = (number_of - 1) // 2
    source_of, taker = lengths[1:1 + 2 * couples:2], lengths[2:2 + 2 * couples:2]
    slack = jnp.minimum(source_of - 1, bound - taker)
    moved = jax.random.randint(jax.random.fold_in(own_key, 1), (couples,), 0, 1 << 20) % (slack + 1)
    lengths = lengths.at[1:1 + 2 * couples:2].set(source_of - moved).at[2:2 + 2 * couples:2].set(taker + moved)
    return lengths[jax.random.permutation(jax.random.fold_in(own_key, 2), number_of)]


def noise(key, dims, width, reach, cuts=(), kind=jnp.bfloat16):
    drawn = jax.random.normal(key, dims, jnp.float32) * width
    if len(cuts) > 0:
        drawn = steps_of(key, dims, cuts, -0.22, 0.18) * drawn
    return jnp.clip(drawn, min=-reach, max=reach).astype(kind)


def setup_inputs(seed: int = 0) -> dict:
    keys = jax.random.split(jax.random.key(seed), 7)
    return {
        "query_rows": draw_query_rows(jax.random.fold_in(keys[6], 71), 0),
        "key_rows": draw_key_rows(jax.random.fold_in(keys[6], 71), 0),
        "value_rows": noise(keys[2], (SEQ, KVH * HD), 3.0, 18.0, ((0, 16),)),
        "out_weight": noise(keys[3], (HQ * HD, D), (HQ * HD // 16) ** -0.5, 0.25, ((0, 16), (1, 16))),
        "block_order": draw_block_order(jax.random.fold_in(keys[6], 71), 0),
        "doc_lengths": uneven(keys[5], NDOC, SEQ, SEQ // 2, 2).astype(jnp.int32),
    }


def locate_all(block_order, doc_lengths):
    storage = jnp.arange(SEQ, dtype=jnp.int32)
    position = (block_order[storage // HALF] * HALF + storage % HALF).astype(jnp.int32)
    doc_ends = jnp.cumsum(doc_lengths).astype(jnp.int32)
    document = jnp.sum((position[:, None] >= doc_ends[None, :]).astype(jnp.int32), axis=1)
    return position, document


def reference(query_rows, key_rows, value_rows, out_weight, block_order, doc_lengths):
    position, document = locate_all(block_order, doc_lengths)
    allowed = (position[None, :] <= position[:, None]) & (document[None, :] == document[:, None])
    grouped = query_rows.reshape(SEQ, KVH, GROUP, HD).transpose(1, 2, 0, 3)
    keyed = key_rows.reshape(SEQ, KVH, HD).transpose(1, 0, 2)
    valued = value_rows.reshape(SEQ, KVH, HD).transpose(1, 0, 2)
    score_scale = HD ** -0.5

    def one_group(operands):
        query_part, key_part, value_part = operands
        key_wide = key_part.astype(jnp.float32)
        value_wide = value_part.astype(jnp.float32)

        def one_head(query_head):
            scores = jnp.einsum('qd,nd->qn', query_head.astype(jnp.float32), key_wide) * score_scale
            scores = jnp.where(allowed, scores, -1e30)
            peak = jnp.max(scores, axis=-1, keepdims=True)
            weights = jnp.where(allowed, jnp.exp(scores - peak), 0.0)
            denominator = jnp.sum(weights, axis=-1)
            rounded = lax.optimization_barrier(weights.astype(jnp.bfloat16)).astype(jnp.float32)
            mixed = jnp.einsum('qn,nd->qd', rounded, value_wide)
            return (mixed / denominator[:, None]).astype(jnp.bfloat16)

        return lax.map(one_head, query_part)

    attended = lax.map(one_group, (grouped, keyed, valued))
    attended = attended.transpose(2, 0, 1, 3).reshape(SEQ, HQ * HD)
    head_block = HQ * HD // N_TP
    split_attn = attended.reshape(SEQ, N_TP, head_block).transpose(1, 0, 2)
    split_weight = out_weight.reshape(N_TP, head_block, D)

    def add_partial(running, operands):
        term = jnp.dot(operands[0], operands[1], preferred_element_type=jnp.float32)
        rounded = lax.optimization_barrier(term.astype(jnp.bfloat16)).astype(jnp.float32)
        return running + rounded, None

    summed, unused = lax.scan(add_partial, jnp.zeros((SEQ, D), jnp.float32), (split_attn, split_weight))
    return summed.astype(jnp.bfloat16)
```

```python
import functools

import jax
import jax.numpy as jnp
from jax import lax
from jax.experimental import pallas as pl
from jax.experimental.pallas import tpu as pltpu
from jax.sharding import PartitionSpec as P

HD = 128
BLK = 192
TILE = 384
HEADS = 4
NZ, NX, NY = 8, 4, 4
SCALE = HD ** (-0.5) * 1.4426950408889634
LOW = -1e30


def flat(z, x, y, c):
    return ((z % 4) * 4 + x) * 16 + y * 4 + (z // 4) * 2 + c


def perm(dz=0, dx=0, dy=0, dc=0):
    pairs = []
    for z in range(NZ):
        for x in range(NX):
            for y in range(NY):
                for c in range(2):
                    to = flat((z + dz) % NZ, (x + dx) % NX, (y + dy) % NY, (c + dc) % 2)
                    pairs.append((flat(z, x, y, c), to))
    return pairs


def send(a, **step):
    return lax.ppermute(a, ("ctx", "tp"), perm(**step))


def attend_kernel(meta, q_ref, mine_ref, theirs_ref, o_ref, ks, vs, m_s, l_s, acc_s):
    ctx = meta[36]
    core = meta[37]
    ks[0:BLK, :] = jnp.zeros((BLK, HD), ks.dtype)
    vs[0:BLK, :] = jnp.zeros((BLK, HD), vs.dtype)

    def place(k_from, v_from):
        for slot in range(16):
            owner = meta[38 + slot]
            for i in range(2):
                at = pl.multiple_of((meta[2 * owner + i] + 1) * BLK, BLK)
                ks[pl.ds(at, BLK), :] = k_from[slot, i * BLK:(i + 1) * BLK, :]
                vs[pl.ds(at, BLK), :] = v_from[slot, i * BLK:(i + 1) * BLK, :]

    @pl.when(core == 0)
    def _():
        place(mine_ref, theirs_ref)

    @pl.when(core != 0)
    def _():
        place(theirs_ref, mine_ref)

    end1 = meta[32]
    end2 = end1 + meta[33]
    end3 = end2 + meta[34]

    def start_of(pos):
        s = jnp.where(pos >= end1, end1, 0)
        s = jnp.where(pos >= end2, end2, s)
        return jnp.where(pos >= end3, end3, s)

    for i in range(2):
        base = meta[2 * ctx + i] * BLK
        top = base + BLK
        low_first = start_of(base)
        low_last = start_of(base + BLK - 1)
        row_pos = base + lax.broadcasted_iota(jnp.int32, (BLK, 1), 0)
        row_start = start_of(row_pos)
        rows = slice(i * BLK, (i + 1) * BLK)

        def scores(t, h, kind):
            first = top - (t + 1) * TILE
            at = pl.multiple_of(first + BLK, BLK)
            k = ks[pl.ds(at, TILE), :]
            s = lax.dot_general(
                q_ref[rows, h * HD:(h + 1) * HD], k, (((1,), (1,)), ((), ())),
                preferred_element_type=jnp.float32,
            ) * SCALE
            if kind != "inner":
                col = first + lax.broadcasted_iota(jnp.int32, (BLK, TILE), 1)
                ok = col >= row_start
                if kind == "diagonal":
                    ok = ok & (col <= row_pos)
                s = jnp.where(ok, s, LOW)
            return s, vs[pl.ds(at, TILE), :]

        for h in range(HEADS):
            s, v = scores(0, h, "diagonal")
            peak = jnp.max(s, axis=1, keepdims=True)
            p = jnp.exp2(s - peak)
            m_s[h] = peak
            l_s[h] = jnp.sum(p, axis=1, keepdims=True)
            acc_s[h] = jnp.dot(p.astype(jnp.bfloat16), v, preferred_element_type=jnp.float32)

        def step(t, kind):
            for h in range(HEADS):
                s, v = scores(t, h, kind)
                old = m_s[h]
                peak = jnp.maximum(old, jnp.max(s, axis=1, keepdims=True))
                fade = jnp.exp2(old - peak)
                p = jnp.exp2(s - peak)
                m_s[h] = peak
                l_s[h] = l_s[h] * fade + jnp.sum(p, axis=1, keepdims=True)
                acc_s[h] = acc_s[h] * fade + jnp.dot(
                    p.astype(jnp.bfloat16), v, preferred_element_type=jnp.float32
                )

        inner = jnp.maximum(1, (top - low_last) // TILE)
        total = (top - low_first + TILE - 1) // TILE

        @pl.loop(1, inner)
        def _(t):
            step(t, "inner")

        @pl.loop(inner, total)
        def _(t):
            step(t, "edge")

        for h in range(HEADS):
            o_ref[rows, h * HD:(h + 1) * HD] = (acc_s[h] / l_s[h]).astype(jnp.bfloat16)


def attend(meta, q, mine, theirs):
    return pl.pallas_call(
        attend_kernel,
        out_shape=jax.ShapeDtypeStruct((2 * BLK, HEADS * HD), jnp.bfloat16),
        in_specs=[pl.BlockSpec(memory_space=pltpu.SMEM)] + [pl.BlockSpec(memory_space=pltpu.VMEM)] * 3,
        out_specs=pl.BlockSpec(memory_space=pltpu.VMEM),
        scratch_shapes=[
            pltpu.VMEM((33 * BLK, HD), jnp.bfloat16),
            pltpu.VMEM((33 * BLK, HD), jnp.bfloat16),
            pltpu.VMEM((HEADS, BLK, 1), jnp.float32),
            pltpu.VMEM((HEADS, BLK, 1), jnp.float32),
            pltpu.VMEM((HEADS, BLK, HD), jnp.float32),
        ],
        compiler_params=pltpu.CompilerParams(vmem_limit_bytes=32 * 2**20),
        cost_estimate=pl.CostEstimate(flops=4 * 10**9, bytes_accessed=4 * 10**6, transcendentals=3 * 10**6),
        name="attend",
    )(meta, q, mine, theirs)


def project_kernel(es, meta, *refs):
    n = len(es)
    a_refs = refs[:2 * n]
    w_own, w_oth = refs[2 * n:2 * n + 2]
    outs = refs[2 * n + 2:2 * n + 6]
    total = refs[2 * n + 6]
    zl, y = meta[0], meta[1]
    for j, e in enumerate(es):
        left, right = a_refs[2 * j], a_refs[2 * j + 1]

        def put(own, oth):
            t = jnp.dot(own[0], w_own[0, 0], preferred_element_type=jnp.float32)
            t += jnp.dot(own[1], w_oth[0, 0], preferred_element_type=jnp.float32)
            t += jnp.dot(oth[0], w_own[0, 1], preferred_element_type=jnp.float32)
            t += jnp.dot(oth[1], w_oth[0, 1], preferred_element_type=jnp.float32)
            total[...] = t

        if e == 0:
            put(left, right)
        else:
            @pl.when(zl + e < 4)
            def _():
                put(left, right)

            @pl.when(zl + e >= 4)
            def _():
                put(right, left)

        for k in range(4):
            at = pl.multiple_of(lax.rem(y + k, 4) * 48, 48)
            outs[k][j] = total[pl.ds(at, 48), :].astype(jnp.bfloat16)


def project(es, meta, pairs, w_own, w_oth):
    n = len(es)
    a_list = [a for pair in pairs for a in pair]
    whole = pl.BlockSpec((2, 192, 512), lambda i: (0, 0, 0))
    w_spec = pl.BlockSpec((1, 2, 512, 512), lambda i: (i, 0, 0, 0))
    return pl.pallas_call(
        functools.partial(project_kernel, es),
        grid=(4,),
        out_shape=[jax.ShapeDtypeStruct((n, 48, 2048), jnp.bfloat16)] * 4,
        in_specs=[pl.BlockSpec(memory_space=pltpu.SMEM)] + [whole] * (2 * n) + [w_spec] * 2,
        out_specs=[pl.BlockSpec((n, 48, 512), lambda i: (0, 0, i))] * 4,
        scratch_shapes=[pltpu.VMEM((192, 512), jnp.float32)],
        compiler_params=pltpu.CompilerParams(vmem_limit_bytes=32 * 2**20),
        cost_estimate=pl.CostEstimate(flops=n * 2 * 192 * 2048 * 2048, bytes_accessed=10**7, transcendentals=0),
        name="project",
    )(meta, *a_list, w_own, w_oth)


def assemble_kernel(meta, *refs):
    out = refs[8]
    z = meta[2]
    for d in range(8):
        src = lax.rem(z + d, 8)
        for x in range(4):
            at = pl.multiple_of((lax.rem(src, 4) * 4 + x) * 1024 + (src // 4) * 512, 512)
            out[:, pl.ds(at, 512)] = refs[d][:, x * 512:(x + 1) * 512]


def assemble(meta, pieces):
    return pl.pallas_call(
        assemble_kernel,
        out_shape=jax.ShapeDtypeStruct((24, 16384), jnp.bfloat16),
        in_specs=[pl.BlockSpec(memory_space=pltpu.SMEM)] + [pl.BlockSpec(memory_space=pltpu.VMEM)] * 8,
        out_specs=pl.BlockSpec(memory_space=pltpu.VMEM),
        name="assemble",
    )(meta, *pieces)


def local(query_rows, key_rows, value_rows, out_weight, block_order, doc_lengths):
    ctx = lax.axis_index("ctx")
    tp = lax.axis_index("tp")
    zl, x = ctx // 4, ctx % 4
    y, zh, core = tp // 4, (tp // 2) % 2, tp % 2
    z = zh * 4 + zl

    def shard_for(zh_to):
        at = (y * 2 + zh_to) * HD
        k = lax.dynamic_slice_in_dim(key_rows, at, HD, 1)
        v = lax.dynamic_slice_in_dim(value_rows, at, HD, 1)
        return jnp.where(core == 0, k, v)

    with jax.named_scope("kv"):
        near = [shard_for(((z + d) % 8) // 4) for d in (0, 1, 7, 2)]
        four = jnp.stack([near[0], send(near[1], dz=1), send(near[2], dz=-1), send(near[3], dz=2)])
        up, down, far = send(four, dx=1), send(four, dx=-1), send(four, dx=2)
        mine = jnp.concatenate([four, up, down, far])
        theirs = send(mine, dc=1)
        steps = [(a, b) for b in (0, -1, 1, 2) for a in (0, -1, 1, 2)]
        owners = [((zl + a + 4) % 4) * 4 + (x + b + 4) % 4 for a, b in steps]
        meta = jnp.concatenate([
            block_order.astype(jnp.int32), doc_lengths.astype(jnp.int32),
            jnp.stack([ctx, core] + owners).astype(jnp.int32),
        ])

    with jax.named_scope("weights"):
        w_keep = lax.dynamic_slice_in_dim(out_weight, zh * 512, 512, 1)
        w_give = lax.dynamic_slice_in_dim(out_weight, (1 - zh) * 512, 512, 1)
        w_pair = jnp.stack([w_keep, send(w_give, dz=4)])
        groups = [[g * 4 + i for i in range(4)] for g in range(4)]
        w_own = lax.all_gather(w_pair, "ctx", axis_index_groups=groups, axis=0, tiled=False)
        w_oth = send(w_own, dc=1)

    with jax.named_scope("attend"):
        attended = attend(meta, query_rows, mine, theirs)

    with jax.named_scope("rows"):
        split = attended.reshape(8, 2, 24, 512)
        keep = lax.dynamic_index_in_dim(split, core, 1, keepdims=False).reshape(192, 512)
        give = lax.dynamic_index_in_dim(split, 1 - core, 1, keepdims=False).reshape(192, 512)
        a0 = jnp.stack([keep, send(give, dc=1)])
        right, left = [a0], [a0]
        for _ in range(3):
            right.append(send(right[-1], dz=1))
            left.append(send(left[-1], dz=-1))
        opposite = jnp.stack([send(right[3][0], dz=1), send(left[3][1], dz=-1)])
        right.append(opposite)
        left.append(opposite)

    where = jnp.stack([zl, y, z]).astype(jnp.int32)
    pieces = [None] * 8
    for es in ((2,), (1, 3), (0,)):
        with jax.named_scope("project"):
            pairs = [(left[e], right[4 - e]) for e in es]
            o = project(es, where, pairs, w_own, w_oth)
        with jax.named_scope("sum"):
            got = [o[0], send(o[1], dy=1), send(o[3], dy=-1), send(o[2], dy=2)]
            summed = sum(g.astype(jnp.float32) for g in got).astype(jnp.bfloat16)
        with jax.named_scope("home"):
            for j, e in enumerate(es):
                part = summed[j].reshape(2, 24, 2048)
                sel = ((z + e) % 8) // 4
                near_part = lax.dynamic_index_in_dim(part, sel, 0, keepdims=False)
                far_part = lax.dynamic_index_in_dim(part, 1 - sel, 0, keepdims=False)
                pieces[(8 - e) % 8] = near_part if e == 0 else send(near_part, dz=e)
                pieces[(12 - e) % 8] = send(far_part, dz=e - 4)
    return assemble(where, pieces)


def solution(mesh):
    in_specs = (P("ctx", "tp"), P("ctx", None), P("ctx", None), P("tp", "ctx"), P(), P())
    out_specs = P(("ctx", "tp"), None)
    return jax.shard_map(local, mesh=mesh, in_specs=in_specs, out_specs=out_specs, check_vma=False)
```

```python
import functools

import jax
import jax.numpy as jnp
from jax import lax
from jax.experimental import pallas as pl
from jax.experimental.pallas import tpu as pltpu
from jax.sharding import PartitionSpec as P

HD = 128
BLK = 192
TILE = 384
HEADS = 4
GROUPS, WIDE = 3, 256
SPLIT = (2, 2)
X_STEPS = (0, 3, 1, 2)
NZ, NX, NY = 8, 4, 4
SCALE = HD ** (-0.5) * 1.4426950408889634
LOW = -1e30


def flat(z, x, y, c):
    return ((z % 4) * 4 + x) * 16 + y * 4 + (z // 4) * 2 + c


def perm(dz=0, dx=0, dy=0, dc=0):
    pairs = []
    for z in range(NZ):
        for x in range(NX):
            for y in range(NY):
                for c in range(2):
                    to = flat((z + dz) % NZ, (x + dx) % NX, (y + dy) % NY, (c + dc) % 2)
                    pairs.append((flat(z, x, y, c), to))
    return pairs


def send(a, **step):
    return lax.ppermute(a, ("ctx", "tp"), perm(**step))


def attend_kernel(meta, q_ref, mine_ref, theirs_ref, *refs):
    o_refs = refs[:4]
    ks, vs, qs, m_s, l_s, acc_s, o_s = refs[4:]
    zh = meta[54]
    ctx = meta[36]
    core = meta[37]
    ks[0:BLK, :] = jnp.zeros((BLK, HD), ks.dtype)
    vs[0:BLK, :] = jnp.zeros((BLK, HD), vs.dtype)

    def place(k_from, v_from):
        for slot in range(16):
            owner = meta[38 + slot]
            for i in range(2):
                at = pl.multiple_of((meta[2 * owner + i] + 1) * BLK, BLK)
                ks[pl.ds(at, BLK), :] = k_from[slot, i * BLK:(i + 1) * BLK, :]
                vs[pl.ds(at, BLK), :] = v_from[slot, i * BLK:(i + 1) * BLK, :]

    @pl.when(core == 0)
    def _():
        place(mine_ref, theirs_ref)

    @pl.when(core != 0)
    def _():
        place(theirs_ref, mine_ref)

    end1 = meta[32]
    end2 = end1 + meta[33]
    end3 = end2 + meta[34]

    def start_of(pos):
        s = jnp.where(pos >= end1, end1, 0)
        s = jnp.where(pos >= end2, end2, s)
        return jnp.where(pos >= end3, end3, s)

    for i in range(2):
        base = meta[2 * ctx + i] * BLK
        top = base + BLK
        low_first = start_of(base)
        low_last = start_of(base + BLK - 1)
        rows = slice(i * BLK, (i + 1) * BLK)
        for h in range(HEADS):
            qs[h * BLK:(h + 1) * BLK, :] = q_ref[rows, h * HD:(h + 1) * HD]

        def scores(t, g, kind):
            first = top - (t + 1) * TILE
            at = pl.multiple_of(first + BLK, BLK)
            s = lax.dot_general(
                ks[pl.ds(at, TILE), :], qs[g * WIDE:(g + 1) * WIDE, :], (((1,), (1,)), ((), ())),
                preferred_element_type=jnp.float32,
            ) * SCALE
            if kind != "inner":
                row = g * WIDE + lax.broadcasted_iota(jnp.int32, (1, WIDE), 1)
                for _ in range(HEADS - 1):
                    row = jnp.where(row >= BLK, row - BLK, row)
                row = row + base
                key = first + lax.broadcasted_iota(jnp.int32, (TILE, WIDE), 0)
                ok = key >= start_of(row)
                if kind == "diagonal":
                    ok = ok & (key <= row)
                s = jnp.where(ok, s, LOW)
            return s, vs[pl.ds(at, TILE), :]

        def mix(v, p):
            return lax.dot_general(
                v, p.astype(jnp.bfloat16), (((0,), (0,)), ((), ())), preferred_element_type=jnp.float32
            )

        for g in range(GROUPS):
            cols = slice(g * WIDE, (g + 1) * WIDE)
            s, v = scores(0, g, "diagonal")
            peak = jnp.max(s, axis=0, keepdims=True)
            p = jnp.exp2(s - peak)
            m_s[:, cols] = peak
            l_s[:, cols] = jnp.sum(p, axis=0, keepdims=True)
            acc_s[:, cols] = mix(v, p)

        def step(t, kind):
            for g in range(GROUPS):
                cols = slice(g * WIDE, (g + 1) * WIDE)
                s, v = scores(t, g, kind)
                old = m_s[:, cols]
                peak = jnp.maximum(old, jnp.max(s, axis=0, keepdims=True))
                fade = jnp.exp2(old - peak)
                p = jnp.exp2(s - peak)
                m_s[:, cols] = peak
                l_s[:, cols] = l_s[:, cols] * fade + jnp.sum(p, axis=0, keepdims=True)
                acc_s[:, cols] = acc_s[:, cols] * fade + mix(v, p)

        inner = jnp.maximum(1, (top - low_last) // TILE)
        total = (top - low_first + TILE - 1) // TILE

        @pl.loop(1, inner)
        def _(t):
            step(t, "inner")

        @pl.loop(inner, total)
        def _(t):
            step(t, "edge")

        o = (acc_s[...] / l_s[...]).T
        for h in range(HEADS):
            for zc in range(4):
                pick = [o[h * BLK + yy * 96 + zc * 24:h * BLK + yy * 96 + (zc + 1) * 24] for yy in range(2)]
                r = (zh + zc // 2) % 2 * 2 + (core + zc % 2) % 2
                o_s[r, i * 48:(i + 1) * 48, h * HD:(h + 1) * HD] = jnp.concatenate(pick).astype(jnp.bfloat16)

    for r in range(4):
        o_refs[r][...] = o_s[r]


def attend(meta, q, mine, theirs):
    return pl.pallas_call(
        attend_kernel,
        out_shape=[jax.ShapeDtypeStruct((96, HEADS * HD), jnp.bfloat16)] * 4,
        in_specs=[pl.BlockSpec(memory_space=pltpu.SMEM)] + [pl.BlockSpec(memory_space=pltpu.VMEM)] * 3,
        out_specs=[pl.BlockSpec(memory_space=pltpu.VMEM)] * 4,
        scratch_shapes=[
            pltpu.VMEM((33 * BLK, HD), jnp.bfloat16),
            pltpu.VMEM((33 * BLK, HD), jnp.bfloat16),
            pltpu.VMEM((HEADS * BLK, HD), jnp.bfloat16),
            pltpu.VMEM((1, HEADS * BLK), jnp.float32),
            pltpu.VMEM((1, HEADS * BLK), jnp.float32),
            pltpu.VMEM((HD, HEADS * BLK), jnp.float32),
            pltpu.VMEM((4, 96, HEADS * HD), jnp.bfloat16),
        ],
        compiler_params=pltpu.CompilerParams(vmem_limit_bytes=32 * 2**20),
        cost_estimate=pl.CostEstimate(flops=4 * 10**9, bytes_accessed=4 * 10**6, transcendentals=3 * 10**6),
        name="attend",
    )(meta, q, mine, theirs)


def project_kernel(meta, *refs):
    a_refs, w_refs, outs = refs[:4], refs[4:8], refs[8:12]
    rows, total = refs[12:]
    y = meta[2]

    @pl.when(pl.program_id(0) == 0)
    def _():
        for i in range(4):
            for r in range(4):
                rows[r, i * 96:(i + 1) * 96, :] = a_refs[i][r]

    t = jnp.dot(rows[0], w_refs[0][0, 0, 0], preferred_element_type=jnp.float32)
    for r in range(1, 4):
        t += jnp.dot(rows[r], w_refs[r][0, 0, 0], preferred_element_type=jnp.float32)
    total[...] = t
    for k in range(4):
        at = lax.rem(y + k, 4) * 24
        four = [total[pl.ds(pl.multiple_of(i * 96 + at, 8), 24), :] for i in range(4)]
        outs[k][...] = jnp.concatenate(four).astype(jnp.bfloat16)


def project(first, count, meta, pieces, w):
    whole = pl.BlockSpec((4, 96, 512), lambda i, m: (0, 0, 0))

    def w_spec(r):
        return pl.BlockSpec(
            (1, 1, 1, 512, 512),
            lambda i, m: ((m[0] + r // 2) % 2, first + i // 2, (m[1] + r % 2) % 2, 0, i % 2),
        )

    with jax.named_scope("project"):
        return pl.pallas_call(
            project_kernel,
            grid_spec=pltpu.PrefetchScalarGridSpec(
                num_scalar_prefetch=1,
                grid=(2 * count,),
                in_specs=[whole] * 4 + [w_spec(r) for r in range(4)],
                out_specs=[pl.BlockSpec((96, 512), lambda i, m: (0, i))] * 4,
                scratch_shapes=[pltpu.VMEM((4, 384, 512), jnp.bfloat16), pltpu.VMEM((384, 512), jnp.float32)],
            ),
            out_shape=[jax.ShapeDtypeStruct((96, count * 1024), jnp.bfloat16)] * 4,
            compiler_params=pltpu.CompilerParams(vmem_limit_bytes=48 * 2**20),
            cost_estimate=pl.CostEstimate(
                flops=count * 2 * 384 * 2048 * 1024, bytes_accessed=count * 5 * 10**6, transcendentals=0),
            name="project",
        )(meta, *pieces, *([w] * 4))


def assemble_kernel(meta, *refs):
    out = refs[-1]
    x = meta[3]
    at_z = 0
    for j, group in enumerate(SPLIT):
        for i, step in enumerate(X_STEPS):
            for g in range(group):
                col = pl.multiple_of(((at_z + g) * 4 + lax.rem(x + step, 4)) * 1024, 1024)
                out[:, pl.ds(col, 1024)] = refs[j * 4 + i][:, g * 1024:(g + 1) * 1024]
        at_z += group


def assemble(meta, pieces):
    return pl.pallas_call(
        assemble_kernel,
        out_shape=jax.ShapeDtypeStruct((24, 16384), jnp.bfloat16),
        in_specs=[pl.BlockSpec(memory_space=pltpu.SMEM)] + [pl.BlockSpec(memory_space=pltpu.VMEM)] * len(pieces),
        out_specs=pl.BlockSpec(memory_space=pltpu.VMEM),
        name="assemble",
    )(meta, *pieces)


def local(query_rows, key_rows, value_rows, out_weight, block_order, doc_lengths):
    ctx = lax.axis_index("ctx")
    tp = lax.axis_index("tp")
    zl, x = ctx // 4, ctx % 4
    y, zh, core = tp // 4, (tp // 2) % 2, tp % 2
    z = zh * 4 + zl

    def shard_for(zh_to):
        at = (y * 2 + zh_to) * HD
        k = lax.dynamic_slice_in_dim(key_rows, at, HD, 1)
        v = lax.dynamic_slice_in_dim(value_rows, at, HD, 1)
        return jnp.where(core == 0, k, v)

    with jax.named_scope("kv"):
        near = [shard_for(((z + d) % 8) // 4) for d in (0, 1, 7, 2)]
        four = jnp.stack([near[0], send(near[1], dz=1), send(near[2], dz=-1), send(near[3], dz=2)])

    with jax.named_scope("weights"):
        groups = [[flat(zz, xx, yy, cc) for zz in range(8) for cc in range(2)] for xx in range(4) for yy in range(4)]
        w = lax.all_gather(out_weight, ("ctx", "tp"), axis_index_groups=groups, axis=0)
        w = w.reshape(2, 4, 2, 512, 1024)

    with jax.named_scope("kv"):
        up, down, far = send(four, dx=1), send(four, dx=-1), send(four, dx=2)
        mine = jnp.concatenate([four, up, down, far])
        theirs = send(mine, dc=1)
        steps = [(a, b) for b in (0, -1, 1, 2) for a in (0, -1, 1, 2)]
        owners = [((zl + a + 4) % 4) * 4 + (x + b + 4) % 4 for a, b in steps]
        meta = jnp.concatenate([
            block_order.astype(jnp.int32), doc_lengths.astype(jnp.int32),
            jnp.stack([ctx, core] + owners + [zh]).astype(jnp.int32),
        ])

    with jax.named_scope("attend"):
        a = attend(meta, query_rows, mine, theirs)

    with jax.named_scope("rows"):
        here = jnp.stack([a[0], send(a[1], dc=1), send(a[2], dz=4), send(a[3], dz=4, dc=1)])
        pieces = [here, send(here, dx=1), send(here, dx=-1), send(here, dx=2)]

    where = jnp.stack([zh, core, y, x]).astype(jnp.int32)
    done = []
    first = 0
    outs = []
    for count in SPLIT:
        outs.append(project(first, count, where, pieces, w))
        first += count
    for o in outs:
        with jax.named_scope("sum"):
            got = [o[0], send(o[1], dy=1), send(o[3], dy=-1), send(o[2], dy=2)]
            total = sum(g.astype(jnp.float32) for g in got).astype(jnp.bfloat16)
        with jax.named_scope("home"):
            own, down, up, far = [total[i * 24:(i + 1) * 24] for i in range(4)]
            up, down = send(up, dx=1), send(down, dx=-1)
            done += [own, up, down, send(far, dx=2)]
    return assemble(where, done)


def solution(mesh):
    in_specs = (P("ctx", "tp"), P("ctx", None), P("ctx", None), P("tp", "ctx"), P(), P())
    out_specs = P(("ctx", "tp"), None)
    return jax.shard_map(local, mesh=mesh, in_specs=in_specs, out_specs=out_specs, check_vma=False)
```

```python
import functools

import jax
import jax.numpy as jnp
from jax import lax
from jax.experimental import pallas as pl
from jax.experimental.pallas import tpu as pltpu
from jax.sharding import PartitionSpec as P

HD = 128
BLK = 192
TILE = 384
HEADS = 4
GROUPS, WIDE = 3, 256
SPLIT = (2, 2)
FLIPS = ((1, 3), (3, 1))
X_STEPS = (0, 3, 1, 2)
NZ, NX, NY = 8, 4, 4
SCALE = HD ** (-0.5) * 1.4426950408889634
LOW = -1e30


def flat(z, x, y, c):
    return ((z % 4) * 4 + x) * 16 + y * 4 + (z // 4) * 2 + c


def perm(dz=0, dx=0, flip=0, dc=0):
    pairs = []
    for z in range(NZ):
        for x in range(NX):
            for y in range(NY):
                for c in range(2):
                    to = flat((z + dz) % NZ, (x + dx) % NX, y ^ flip, (c + dc) % 2)
                    pairs.append((flat(z, x, y, c), to))
    return pairs


def send(a, **step):
    return lax.ppermute(a, ("ctx", "tp"), perm(**step))


def attend_kernel(meta, q_ref, mine_ref, theirs_ref, *refs):
    o_refs = refs[:4]
    ks, vs, qs, m_s, l_s, acc_s, o_s = refs[4:]
    zh = meta[54]
    ctx = meta[36]
    core = meta[37]
    ks[0:BLK, :] = jnp.zeros((BLK, HD), ks.dtype)
    vs[0:BLK, :] = jnp.zeros((BLK, HD), vs.dtype)

    def place(k_from, v_from):
        for slot in range(16):
            owner = meta[38 + slot]
            for i in range(2):
                at = pl.multiple_of((meta[2 * owner + i] + 1) * BLK, BLK)
                ks[pl.ds(at, BLK), :] = k_from[slot, i * BLK:(i + 1) * BLK, :]
                vs[pl.ds(at, BLK), :] = v_from[slot, i * BLK:(i + 1) * BLK, :]

    @pl.when(core == 0)
    def _():
        place(mine_ref, theirs_ref)

    @pl.when(core != 0)
    def _():
        place(theirs_ref, mine_ref)

    end1 = meta[32]
    end2 = end1 + meta[33]
    end3 = end2 + meta[34]

    def start_of(pos):
        s = jnp.where(pos >= end1, end1, 0)
        s = jnp.where(pos >= end2, end2, s)
        return jnp.where(pos >= end3, end3, s)

    for i in range(2):
        base = meta[2 * ctx + i] * BLK
        top = base + BLK
        low_first = start_of(base)
        low_last = start_of(base + BLK - 1)
        rows = slice(i * BLK, (i + 1) * BLK)
        for h in range(HEADS):
            qs[h * BLK:(h + 1) * BLK, :] = q_ref[rows, h * HD:(h + 1) * HD]

        def scores(t, g, kind):
            first = top - (t + 1) * TILE
            at = pl.multiple_of(first + BLK, BLK)
            s = lax.dot_general(
                ks[pl.ds(at, TILE), :], qs[g * WIDE:(g + 1) * WIDE, :], (((1,), (1,)), ((), ())),
                preferred_element_type=jnp.float32,
            ) * SCALE
            if kind != "inner":
                row = g * WIDE + lax.broadcasted_iota(jnp.int32, (1, WIDE), 1)
                for _ in range(HEADS - 1):
                    row = jnp.where(row >= BLK, row - BLK, row)
                row = row + base
                key = first + lax.broadcasted_iota(jnp.int32, (TILE, WIDE), 0)
                ok = key >= start_of(row)
                if kind == "diagonal":
                    ok = ok & (key <= row)
                s = jnp.where(ok, s, LOW)
            return s, vs[pl.ds(at, TILE), :]

        def mix(v, p):
            return lax.dot_general(
                v, p.astype(jnp.bfloat16), (((0,), (0,)), ((), ())), preferred_element_type=jnp.float32
            )

        for g in range(GROUPS):
            cols = slice(g * WIDE, (g + 1) * WIDE)
            s, v = scores(0, g, "diagonal")
            peak = jnp.max(s, axis=0, keepdims=True)
            p = jnp.exp2(s - peak)
            m_s[:, cols] = peak
            l_s[:, cols] = jnp.sum(p, axis=0, keepdims=True)
            acc_s[:, cols] = mix(v, p)

        def step(t, kind):
            for g in range(GROUPS):
                cols = slice(g * WIDE, (g + 1) * WIDE)
                s, v = scores(t, g, kind)
                old = m_s[:, cols]
                peak = jnp.maximum(old, jnp.max(s, axis=0, keepdims=True))
                fade = jnp.exp2(old - peak)
                p = jnp.exp2(s - peak)
                m_s[:, cols] = peak
                l_s[:, cols] = l_s[:, cols] * fade + jnp.sum(p, axis=0, keepdims=True)
                acc_s[:, cols] = acc_s[:, cols] * fade + mix(v, p)

        inner = jnp.maximum(1, (top - low_last) // TILE)
        total = (top - low_first + TILE - 1) // TILE

        @pl.loop(1, inner)
        def _(t):
            step(t, "inner")

        @pl.loop(inner, total)
        def _(t):
            step(t, "edge")

        o = (acc_s[...] / l_s[...]).T
        for h in range(HEADS):
            for zc in range(4):
                pick = [o[h * BLK + yy * 96 + zc * 24:h * BLK + yy * 96 + (zc + 1) * 24] for yy in range(2)]
                r = (zh + zc // 2) % 2 * 2 + (core + zc % 2) % 2
                o_s[r, i * 48:(i + 1) * 48, h * HD:(h + 1) * HD] = jnp.concatenate(pick).astype(jnp.bfloat16)

    for r in range(4):
        o_refs[r][...] = o_s[r]


def attend(meta, q, mine, theirs):
    return pl.pallas_call(
        attend_kernel,
        out_shape=[jax.ShapeDtypeStruct((96, HEADS * HD), jnp.bfloat16)] * 4,
        in_specs=[pl.BlockSpec(memory_space=pltpu.SMEM)] + [pl.BlockSpec(memory_space=pltpu.VMEM)] * 3,
        out_specs=[pl.BlockSpec(memory_space=pltpu.VMEM)] * 4,
        scratch_shapes=[
            pltpu.VMEM((33 * BLK, HD), jnp.bfloat16),
            pltpu.VMEM((33 * BLK, HD), jnp.bfloat16),
            pltpu.VMEM((HEADS * BLK, HD), jnp.bfloat16),
            pltpu.VMEM((1, HEADS * BLK), jnp.float32),
            pltpu.VMEM((1, HEADS * BLK), jnp.float32),
            pltpu.VMEM((HD, HEADS * BLK), jnp.float32),
            pltpu.VMEM((4, 96, HEADS * HD), jnp.bfloat16),
        ],
        compiler_params=pltpu.CompilerParams(vmem_limit_bytes=32 * 2**20),
        cost_estimate=pl.CostEstimate(flops=4 * 10**9, bytes_accessed=4 * 10**6, transcendentals=3 * 10**6),
        name="attend",
    )(meta, q, mine, theirs)


def project_kernel(meta, *refs):
    a_refs, w_refs, outs = refs[:4], refs[4:8], refs[8:12]
    rows, total = refs[12:]
    y = meta[2]

    @pl.when(pl.program_id(0) == 0)
    def _():
        for i in range(4):
            for r in range(4):
                rows[r, i * 96:(i + 1) * 96, :] = a_refs[i][r]

    t = jnp.dot(rows[0], w_refs[0][0, 0, 0], preferred_element_type=jnp.float32)
    for r in range(1, 4):
        t += jnp.dot(rows[r], w_refs[r][0, 0, 0], preferred_element_type=jnp.float32)
    total[...] = t
    for h, (a, b) in enumerate(FLIPS):
        for out, first in ((outs[2 * h], a), (outs[2 * h + 1], 0)):
            for k, flip in enumerate((first, first ^ b)):
                at = lax.bitwise_xor(y, flip) * 24
                four = [
                    total[pl.ds(pl.multiple_of(i * 96 + at, 8), 24), h * 512:(h + 1) * 512] for i in range(4)
                ]
                out[k] = jnp.concatenate(four).astype(jnp.bfloat16)


def project(first, count, meta, pieces, w):
    whole = pl.BlockSpec((4, 96, 512), lambda i, m: (0, 0, 0))

    def w_spec(r):
        return pl.BlockSpec(
            (1, 1, 1, 512, 1024),
            lambda i, m: ((m[0] + r // 2) % 2, first + i, (m[1] + r % 2) % 2, 0, 0),
        )

    with jax.named_scope("project"):
        return pl.pallas_call(
            project_kernel,
            grid_spec=pltpu.PrefetchScalarGridSpec(
                num_scalar_prefetch=1,
                grid=(count,),
                in_specs=[whole] * 4 + [w_spec(r) for r in range(4)],
                out_specs=[pl.BlockSpec((2, 96, 512), lambda i, m: (0, 0, i))] * 4,
                scratch_shapes=[pltpu.VMEM((4, 384, 512), jnp.bfloat16), pltpu.VMEM((384, 1024), jnp.float32)],
            ),
            out_shape=[jax.ShapeDtypeStruct((2, 96, count * 512), jnp.bfloat16)] * 4,
            compiler_params=pltpu.CompilerParams(vmem_limit_bytes=48 * 2**20),
            cost_estimate=pl.CostEstimate(
                flops=count * 2 * 384 * 2048 * 1024, bytes_accessed=count * 5 * 10**6, transcendentals=0),
            name="project",
        )(meta, *pieces, *([w] * 4))


def assemble_kernel(meta, *refs):
    out = refs[-1]
    x = meta[3]
    at_z = 0
    for j, group in enumerate(SPLIT):
        for i, step in enumerate(X_STEPS):
            for g in range(group):
                for h in range(2):
                    col = pl.multiple_of(((at_z + g) * 4 + lax.rem(x + step, 4)) * 1024 + h * 512, 512)
                    at = (h * group + g) * 512
                    out[:, pl.ds(col, 512)] = refs[j * 4 + i][:, at:at + 512]
        at_z += group


def assemble(meta, pieces):
    return pl.pallas_call(
        assemble_kernel,
        out_shape=jax.ShapeDtypeStruct((24, 16384), jnp.bfloat16),
        in_specs=[pl.BlockSpec(memory_space=pltpu.SMEM)] + [pl.BlockSpec(memory_space=pltpu.VMEM)] * len(pieces),
        out_specs=pl.BlockSpec(memory_space=pltpu.VMEM),
        name="assemble",
    )(meta, *pieces)


def local(query_rows, key_rows, value_rows, out_weight, block_order, doc_lengths):
    ctx = lax.axis_index("ctx")
    tp = lax.axis_index("tp")
    zl, x = ctx // 4, ctx % 4
    y, zh, core = tp // 4, (tp // 2) % 2, tp % 2
    z = zh * 4 + zl

    def shard_for(zh_to):
        at = (y * 2 + zh_to) * HD
        k = lax.dynamic_slice_in_dim(key_rows, at, HD, 1)
        v = lax.dynamic_slice_in_dim(value_rows, at, HD, 1)
        return jnp.where(core == 0, k, v)

    with jax.named_scope("kv"):
        near = [shard_for(((z + d) % 8) // 4) for d in (0, 1, 7, 2)]
        four = jnp.stack([near[0], send(near[1], dz=1), send(near[2], dz=-1), send(near[3], dz=2)])

    with jax.named_scope("weights"):
        groups = [[flat(zz, xx, yy, cc) for zz in range(8) for cc in range(2)] for xx in range(4) for yy in range(4)]
        w = lax.all_gather(out_weight, ("ctx", "tp"), axis_index_groups=groups, axis=0)
        w = w.reshape(2, 4, 2, 512, 1024)

    with jax.named_scope("kv"):
        up, down, far = send(four, dx=1), send(four, dx=-1), send(four, dx=2)
        mine = jnp.concatenate([four, up, down, far])
        theirs = send(mine, dc=1)
        steps = [(a, b) for b in (0, -1, 1, 2) for a in (0, -1, 1, 2)]
        owners = [((zl + a + 4) % 4) * 4 + (x + b + 4) % 4 for a, b in steps]
        meta = jnp.concatenate([
            block_order.astype(jnp.int32), doc_lengths.astype(jnp.int32),
            jnp.stack([ctx, core] + owners + [zh]).astype(jnp.int32),
        ])

    with jax.named_scope("attend"):
        a = attend(meta, query_rows, mine, theirs)

    with jax.named_scope("rows"):
        here = jnp.stack([a[0], send(a[1], dc=1), send(a[2], dz=4), send(a[3], dz=4, dc=1)])
        pieces = [here, send(here, dx=1), send(here, dx=-1), send(here, dx=2)]

    where = jnp.stack([zh, core, y, x]).astype(jnp.int32)
    done = []
    first = 0
    outs = []
    for count in SPLIT:
        outs.append(project(first, count, where, pieces, w))
        first += count
    for o in outs:
        with jax.named_scope("sum"):
            halves = []
            for h, (a, b) in enumerate(FLIPS):
                got, kept = send(o[2 * h], flip=a).astype(jnp.float32), o[2 * h + 1].astype(jnp.float32)
                last = send((kept[1] + got[1]).astype(jnp.bfloat16), flip=b)
                halves.append((kept[0] + got[0] + last.astype(jnp.float32)).astype(jnp.bfloat16))
            total = jnp.concatenate(halves, axis=1)
        with jax.named_scope("home"):
            own, down, up, far = [total[i * 24:(i + 1) * 24] for i in range(4)]
            up, down = send(up, dx=1), send(down, dx=-1)
            done += [own, up, down, send(far, dx=2)]
    return assemble(where, done)


def solution(mesh):
    in_specs = (P("ctx", "tp"), P("ctx", None), P("ctx", None), P("tp", "ctx"), P(), P())
    out_specs = P(("ctx", "tp"), None)
    return jax.shard_map(local, mesh=mesh, in_specs=in_specs, out_specs=out_specs, check_vma=False)
```

```python
import functools

import jax
import jax.numpy as jnp
from jax import lax
from jax.experimental import pallas as pl
from jax.experimental.pallas import tpu as pltpu
from jax.sharding import PartitionSpec as P

HD = 128
BLK = 192
TILE = 384
HEADS = 4
GROUPS, WIDE = 3, 256
SPLIT = (2, 2)
FLIPS = ((1, 3), (3, 1))
X_STEPS = (0, 3, 1, 2)
NZ, NX, NY = 8, 4, 4
SCALE = HD ** (-0.5) * 1.4426950408889634
LOW = -1e30


def flat(z, x, y, c):
    return ((z % 4) * 4 + x) * 16 + y * 4 + (z // 4) * 2 + c


def perm(dz=0, dx=0, flip=0, dc=0):
    pairs = []
    for z in range(NZ):
        for x in range(NX):
            for y in range(NY):
                for c in range(2):
                    to = flat((z + dz) % NZ, (x + dx) % NX, y ^ flip, (c + dc) % 2)
                    pairs.append((flat(z, x, y, c), to))
    return pairs


def send(a, **step):
    return lax.ppermute(a, ("ctx", "tp"), perm(**step))


def attend_kernel(meta, q_ref, mine_ref, theirs_ref, *refs):
    o_refs = refs[:4]
    ks, vs, qs, m_s, l_s, acc_s, o_s = refs[4:]
    zh = meta[54]
    ctx = meta[36]
    core = meta[37]
    ks[0:BLK, :] = jnp.zeros((BLK, HD), ks.dtype)
    vs[0:BLK, :] = jnp.zeros((BLK, HD), vs.dtype)

    def place(k_from, v_from):
        for slot in range(16):
            owner = meta[38 + slot]
            for i in range(2):
                at = pl.multiple_of((meta[2 * owner + i] + 1) * BLK, BLK)
                ks[pl.ds(at, BLK), :] = k_from[slot, i * BLK:(i + 1) * BLK, :]
                vs[pl.ds(at, BLK), :] = v_from[slot, i * BLK:(i + 1) * BLK, :]

    @pl.when(core == 0)
    def _():
        place(mine_ref, theirs_ref)

    @pl.when(core != 0)
    def _():
        place(theirs_ref, mine_ref)

    end1 = meta[32]
    end2 = end1 + meta[33]
    end3 = end2 + meta[34]

    def start_of(pos):
        s = jnp.where(pos >= end1, end1, 0)
        s = jnp.where(pos >= end2, end2, s)
        return jnp.where(pos >= end3, end3, s)

    for i in range(2):
        base = meta[2 * ctx + i] * BLK
        top = base + BLK
        low_first = start_of(base)
        low_last = start_of(base + BLK - 1)
        rows = slice(i * BLK, (i + 1) * BLK)
        for h in range(HEADS):
            qs[h * BLK:(h + 1) * BLK, :] = q_ref[rows, h * HD:(h + 1) * HD]

        def scores(t, g, kind):
            first = top - (t + 1) * TILE
            at = pl.multiple_of(first + BLK, BLK)
            s = lax.dot_general(
                ks[pl.ds(at, TILE), :], qs[g * WIDE:(g + 1) * WIDE, :], (((1,), (1,)), ((), ())),
                preferred_element_type=jnp.float32,
            ) * SCALE
            if kind != "inner":
                row = g * WIDE + lax.broadcasted_iota(jnp.int32, (1, WIDE), 1)
                for _ in range(HEADS - 1):
                    row = jnp.where(row >= BLK, row - BLK, row)
                row = row + base
                key = first + lax.broadcasted_iota(jnp.int32, (TILE, WIDE), 0)
                ok = key >= start_of(row)
                if kind == "diagonal":
                    ok = ok & (key <= row)
                s = jnp.where(ok, s, LOW)
            return s, vs[pl.ds(at, TILE), :]

        def mix(v, p):
            return lax.dot_general(
                v, p.astype(jnp.bfloat16), (((0,), (0,)), ((), ())), preferred_element_type=jnp.float32
            )

        for g in range(GROUPS):
            cols = slice(g * WIDE, (g + 1) * WIDE)
            s, v = scores(0, g, "diagonal")
            peak = jnp.max(s, axis=0, keepdims=True)
            p = jnp.exp2(s - peak)
            m_s[:, cols] = peak
            l_s[:, cols] = jnp.sum(p, axis=0, keepdims=True)
            acc_s[:, cols] = mix(v, p)

        def step(t, kind):
            for g in range(GROUPS):
                cols = slice(g * WIDE, (g + 1) * WIDE)
                s, v = scores(t, g, kind)
                old = m_s[:, cols]
                peak = jnp.maximum(old, jnp.max(s, axis=0, keepdims=True))
                fade = jnp.exp2(old - peak)
                p = jnp.exp2(s - peak)
                m_s[:, cols] = peak
                l_s[:, cols] = l_s[:, cols] * fade + jnp.sum(p, axis=0, keepdims=True)
                acc_s[:, cols] = acc_s[:, cols] * fade + mix(v, p)

        inner = jnp.maximum(1, (top - low_last) // TILE)
        total = (top - low_first + TILE - 1) // TILE

        @pl.loop(1, inner)
        def _(t):
            step(t, "inner")

        @pl.loop(inner, total)
        def _(t):
            step(t, "edge")

        o = (acc_s[...] / l_s[...]).T
        for h in range(HEADS):
            for zc in range(4):
                pick = [o[h * BLK + yy * 96 + zc * 24:h * BLK + yy * 96 + (zc + 1) * 24] for yy in range(2)]
                r = (zh + zc // 2) % 2 * 2 + (core + zc % 2) % 2
                o_s[r, i * 48:(i + 1) * 48, h * HD:(h + 1) * HD] = jnp.concatenate(pick).astype(jnp.bfloat16)

    for r in range(4):
        o_refs[r][...] = o_s[r]


def attend(meta, q, mine, theirs):
    return pl.pallas_call(
        attend_kernel,
        out_shape=[jax.ShapeDtypeStruct((96, HEADS * HD), jnp.bfloat16)] * 4,
        in_specs=[pl.BlockSpec(memory_space=pltpu.SMEM)] + [pl.BlockSpec(memory_space=pltpu.VMEM)] * 3,
        out_specs=[pl.BlockSpec(memory_space=pltpu.VMEM)] * 4,
        scratch_shapes=[
            pltpu.VMEM((33 * BLK, HD), jnp.bfloat16),
            pltpu.VMEM((33 * BLK, HD), jnp.bfloat16),
            pltpu.VMEM((HEADS * BLK, HD), jnp.bfloat16),
            pltpu.VMEM((1, HEADS * BLK), jnp.float32),
            pltpu.VMEM((1, HEADS * BLK), jnp.float32),
            pltpu.VMEM((HD, HEADS * BLK), jnp.float32),
            pltpu.VMEM((4, 96, HEADS * HD), jnp.bfloat16),
        ],
        compiler_params=pltpu.CompilerParams(vmem_limit_bytes=32 * 2**20),
        cost_estimate=pl.CostEstimate(flops=4 * 10**9, bytes_accessed=4 * 10**6, transcendentals=3 * 10**6),
        name="attend",
    )(meta, q, mine, theirs)


def project_kernel(meta, *refs):
    a_refs, w_ref, outs = refs[:4], refs[4], refs[5:9]
    rows, total = refs[9:]
    zh, core, y = meta[0], meta[1], meta[2]

    @pl.when(pl.program_id(0) == 0)
    def _():
        for r in range(4):
            at = pl.multiple_of((lax.rem(zh + r // 2, 2) * 2 + lax.rem(core + r % 2, 2)) * 512, 512)
            for i in range(4):
                rows[i * 96:(i + 1) * 96, pl.ds(at, 512)] = a_refs[i][r]

    w = w_ref[...].reshape(2048, 1024)
    total[...] = jnp.dot(rows[...], w, preferred_element_type=jnp.float32)
    for h, (a, b) in enumerate(FLIPS):
        for out, first in ((outs[2 * h], a), (outs[2 * h + 1], 0)):
            for k, flip in enumerate((first, first ^ b)):
                at = lax.bitwise_xor(y, flip) * 24
                four = [
                    total[pl.ds(pl.multiple_of(i * 96 + at, 8), 24), h * 512:(h + 1) * 512] for i in range(4)
                ]
                out[k] = jnp.concatenate(four).astype(jnp.bfloat16)


def project(first, count, meta, pieces, w):
    whole = pl.BlockSpec((4, 96, 512), lambda i, m: (0, 0, 0))

    w_spec = pl.BlockSpec((2, 1, 2, 512, 1024), lambda i, m: (0, first + i, 0, 0, 0))

    with jax.named_scope("project"):
        return pl.pallas_call(
            project_kernel,
            grid_spec=pltpu.PrefetchScalarGridSpec(
                num_scalar_prefetch=1,
                grid=(count,),
                in_specs=[whole] * 4 + [w_spec],
                out_specs=[pl.BlockSpec((2, 96, 512), lambda i, m: (0, 0, i))] * 4,
                scratch_shapes=[pltpu.VMEM((384, 2048), jnp.bfloat16), pltpu.VMEM((384, 1024), jnp.float32)],
            ),
            out_shape=[jax.ShapeDtypeStruct((2, 96, count * 512), jnp.bfloat16)] * 4,
            compiler_params=pltpu.CompilerParams(vmem_limit_bytes=48 * 2**20),
            cost_estimate=pl.CostEstimate(
                flops=count * 2 * 384 * 2048 * 1024, bytes_accessed=count * 5 * 10**6, transcendentals=0),
            name="project",
        )(meta, *pieces, w)


def assemble_kernel(meta, *refs):
    out = refs[-1]
    x = meta[3]
    at_z = 0
    for group in SPLIT:
        for i, step in enumerate(X_STEPS):
            for g in range(group):
                for h in range(2):
                    col = pl.multiple_of(((at_z + g) * 4 + lax.rem(x + step, 4)) * 1024 + h * 512, 512)
                    at = (2 * at_z + h * group + g) * 512
                    out[:, pl.ds(col, 512)] = refs[i][:, at:at + 512]
        at_z += group


def assemble(meta, pieces):
    return pl.pallas_call(
        assemble_kernel,
        out_shape=jax.ShapeDtypeStruct((24, 16384), jnp.bfloat16),
        in_specs=[pl.BlockSpec(memory_space=pltpu.SMEM)] + [pl.BlockSpec(memory_space=pltpu.VMEM)] * len(pieces),
        out_specs=pl.BlockSpec(memory_space=pltpu.VMEM),
        compiler_params=pltpu.CompilerParams(vmem_limit_bytes=56 * 2**20),
        name="assemble",
    )(meta, *pieces)


def local(query_rows, key_rows, value_rows, out_weight, block_order, doc_lengths):
    ctx = lax.axis_index("ctx")
    tp = lax.axis_index("tp")
    zl, x = ctx // 4, ctx % 4
    y, zh, core = tp // 4, (tp // 2) % 2, tp % 2
    z = zh * 4 + zl

    def shard_for(zh_to):
        at = (y * 2 + zh_to) * HD
        k = lax.dynamic_slice_in_dim(key_rows, at, HD, 1)
        v = lax.dynamic_slice_in_dim(value_rows, at, HD, 1)
        return jnp.where(core == 0, k, v)

    with jax.named_scope("kv"):
        near = [shard_for(((z + d) % 8) // 4) for d in (0, 1, 7, 2)]
        four = jnp.stack([near[0], send(near[1], dz=1), send(near[2], dz=-1), send(near[3], dz=2)])

    with jax.named_scope("weights"):
        groups = [[flat(zz, xx, yy, cc) for zz in range(8) for cc in range(2)] for xx in range(4) for yy in range(4)]
        w = lax.all_gather(out_weight, ("ctx", "tp"), axis_index_groups=groups, axis=0)
        w = w.reshape(2, 4, 2, 512, 1024)

    with jax.named_scope("kv"):
        up, down, far = send(four, dx=1), send(four, dx=-1), send(four, dx=2)
        mine = jnp.concatenate([four, up, down, far])
        theirs = send(mine, dc=1)
        steps = [(a, b) for b in (0, -1, 1, 2) for a in (0, -1, 1, 2)]
        owners = [((zl + a + 4) % 4) * 4 + (x + b + 4) % 4 for a, b in steps]
        meta = jnp.concatenate([
            block_order.astype(jnp.int32), doc_lengths.astype(jnp.int32),
            jnp.stack([ctx, core] + owners + [zh]).astype(jnp.int32),
        ])

    with jax.named_scope("attend"):
        a = attend(meta, query_rows, mine, theirs)

    with jax.named_scope("rows"):
        here = jnp.stack([a[0], send(a[1], dc=1), send(a[2], dz=4), send(a[3], dz=4, dc=1)])
        pieces = [here, send(here, dx=1), send(here, dx=-1), send(here, dx=2)]

    where = jnp.stack([zh, core, y, x]).astype(jnp.int32)
    done = []
    first = 0
    outs = []
    for count in SPLIT:
        outs.append(project(first, count, where, pieces, w))
        first += count
    for o in outs:
        with jax.named_scope("sum"):
            halves = []
            for h, (a, b) in enumerate(FLIPS):
                got, kept = send(o[2 * h], flip=a).astype(jnp.float32), o[2 * h + 1].astype(jnp.float32)
                last = send((kept[1] + got[1]).astype(jnp.bfloat16), flip=b)
                halves.append((kept[0] + got[0] + last.astype(jnp.float32)).astype(jnp.bfloat16))
            total = jnp.concatenate(halves, axis=1)
        done.append(total)
    with jax.named_scope("home"):
        total = jnp.concatenate(done, axis=1)
        own, down, up, far = [total[i * 24:(i + 1) * 24] for i in range(4)]
        up, down = send(up, dx=1), send(down, dx=-1)
        done = [own, up, down, send(far, dx=2)]
    return assemble(where, done)


def solution(mesh):
    in_specs = (P("ctx", "tp"), P("ctx", None), P("ctx", None), P("tp", "ctx"), P(), P())
    out_specs = P(("ctx", "tp"), None)
    return jax.shard_map(local, mesh=mesh, in_specs=in_specs, out_specs=out_specs, check_vma=False)
```
